32 devices in a mesh: dp: 8 (over z, x), fsdp: 4 (over y, core).
Axes of the slice: x: 2, y: 2, z: 4, core: 2. Of those that a mesh axis runs over, the one named last changes fastest.
Arguments:
- frames: bfloat16 [8, 4, 576, 1024], P('dp', 'fsdp'), may hold values from -6 to 6
- route: int32 [8, 4, 576], P('dp', 'fsdp'), may hold values from 0 to 575, each once within a row
- valid: int32 [8, 4, 576], P('dp', 'fsdp'), may hold values 0 or 1
- w_pw: bfloat16 [1024, 2048], P('fsdp'), may hold values from -0.1875 to 0.1875
- cotangent: bfloat16 [8, 4, 576, 1024], P('dp', 'fsdp'), may hold values from -6 to 6
Outputs:
- gated: bfloat16 [8, 4, 576, 1024], P('dp', 'fsdp')
- grad_pw: bfloat16 [8, 1024, 2048], P('dp', 'fsdp')
The draws below stay inside these ranges and needn't reach their ends.
Inputs may be any that keep to these rules, and one draw needn't show every extreme that they name: Each row of route is a permutation of the frames of one device.
All inputs are finite; a program needn't handle non-finite values. No bound on the sum of `valid` on one device may be relied on, other than what follows from the above.
Results may differ from the reference program's by a relative error of at most 0.017.
Values may be sent and summed in bfloat16 or wider, within the bound.
A program may use at most 64 MiB of HBM per device.

```python
import jax
import jax.numpy as jnp
from jax import lax

D = 1024
ROWS_DEV = 576
N_DP = 8
N_FSDP = 4


def touch_ends(drawn, key, smallest, largest):
    spot = [jax.random.randint(jax.random.fold_in(key, axis), (), 0, length) for axis, length in enumerate(drawn.shape)]
    main_axis = drawn.shape.index(max(drawn.shape))
    neighbour = spot[:main_axis] + [(spot[main_axis] + 1) % drawn.shape[main_axis]] + spot[main_axis + 1:]
    return drawn.at[tuple(spot)].set(smallest).at[tuple(neighbour)].set(largest)


def block_scale(stream_key, shape, cuts, least, high):
    def one(position, shards_of):
        steps = jax.random.uniform(jax.random.fold_in(jax.random.fold_in(stream_key, 6), position), (shards_of,), jnp.float32, least / len(cuts), high / len(cuts))
        return jnp.repeat(jnp.exp(steps), shape[position] // shards_of).reshape((-1,) + (1,) * (len(shape) - position - 1))

    factor_of = one(*cuts[0])
    for cut in cuts[1:]:
        factor_of = factor_of * one(*cut)
    return factor_of


def scatter_about(key, shape, scale, reach, split=(), kind=jnp.bfloat16):
    array = scale * jax.random.normal(key, shape, jnp.float32)
    if split:
        array = array * block_scale(key, shape, split, -0.22, 0.18)
    return jnp.clip(array, -reach, reach).astype(kind)


def setup_inputs(seed: int = 0) -> dict:
    arg_keys = jax.random.split(jax.random.key(seed), 6)
    return {
        "frames": scatter_about(arg_keys[0], (N_DP, N_FSDP, ROWS_DEV, D), 1.0, 6.0, ((0, 8), (1, 4))),
        "route": jax.vmap(lambda own: jax.random.permutation(own, ROWS_DEV))(jax.random.split(arg_keys[1], N_DP * N_FSDP)).reshape((N_DP, N_FSDP, ROWS_DEV)).astype(jnp.int32),
        "valid": touch_ends((jax.random.randint(arg_keys[2], (N_DP, N_FSDP, ROWS_DEV), 0, 4) < 3).astype(jnp.int32), jax.random.fold_in(arg_keys[2], 1), 0, 1),
        "w_pw": scatter_about(arg_keys[3], (D, 2 * D), D ** -0.5, 0.1875, ((0, 4),)),
        "cotangent": scatter_about(arg_keys[4], (N_DP, N_FSDP, ROWS_DEV, D), 1.0, 6.0, ((0, 8), (1, 4))),
    }


def reference(frames, route, valid, w_pw, cotangent):
    picked = jnp.take_along_axis(frames, route[..., None], axis=2)
    keep = jnp.take_along_axis(valid, route, axis=2)
    sent = jnp.where(keep[..., None] > 0, picked, jnp.zeros_like(picked)).astype(jnp.bfloat16)
    width = frames.shape[3]
    blocks = sent.reshape(N_DP, N_FSDP, N_DP, ROWS_DEV // N_DP, width)
    received = jnp.transpose(blocks, (2, 1, 0, 3, 4)).reshape(N_DP, N_FSDP, ROWS_DEV, width)

    def group(pair):
        rows, grads = pair
        values = rows.astype(jnp.float32)
        mean = lax.optimization_barrier(jnp.mean(values, axis=-1, keepdims=True))
        centred = values - mean
        variance = lax.optimization_barrier(jnp.mean(centred * centred, axis=-1, keepdims=True))
        normed = (centred * lax.rsqrt(variance + 1e-05)).astype(jnp.bfloat16)
        flat = normed.reshape(N_FSDP * ROWS_DEV, width)
        pre = jnp.dot(flat, w_pw, preferred_element_type=jnp.float32)
        first = pre[:, :width]
        second = jax.nn.sigmoid(pre[:, width:])
        gated = (first * second).astype(jnp.bfloat16)
        upstream = grads.reshape(N_FSDP * ROWS_DEV, width).astype(jnp.float32)
        dpre = jnp.concatenate([upstream * second, upstream * first * second * (1.0 - second)], axis=1).astype(jnp.bfloat16)
        total = jnp.zeros((width, 2 * width), jnp.float32)
        for index in range(N_FSDP):
            lower = index * ROWS_DEV
            part = lax.dot_general(flat[lower:lower + ROWS_DEV], dpre[lower:lower + ROWS_DEV], (((0,), (0,)), ((), ())), preferred_element_type=jnp.float32)
            total = total + part.astype(jnp.bfloat16).astype(jnp.float32)
        return (gated.reshape(N_FSDP, ROWS_DEV, width), total.astype(jnp.bfloat16))
    gated, grad_pw = lax.map(group, (received, cotangent))
    return (gated, grad_pw)
```

```python
import functools

import jax
import jax.numpy as jnp
from jax import lax
from jax.experimental import pallas as pl
from jax.experimental.pallas import tpu as pltpu
from jax.sharding import PartitionSpec as P

TILE = 256
W_PARTS = 4


def plain(frames, route, valid, w_pw, cotangent):
    width = frames.shape[3]
    local = frames[0, 0]
    order = route[0, 0]
    picked = jnp.take(local, order, axis=0)
    keep = jnp.take(valid[0, 0], order, axis=0)
    sent = jnp.where(keep[:, None] > 0, picked, jnp.zeros_like(picked))
    received = lax.all_to_all(sent, "dp", split_axis=0, concat_axis=0, tiled=True)
    values = received.astype(jnp.float32)
    mean = jnp.mean(values, axis=-1, keepdims=True)
    centred = values - mean
    variance = jnp.mean(centred * centred, axis=-1, keepdims=True)
    normed = (centred * lax.rsqrt(variance + 1e-05)).astype(jnp.bfloat16)
    pre = jnp.dot(
        normed,
        lax.all_gather(w_pw, "fsdp", axis=0, tiled=True),
        preferred_element_type=jnp.float32,
    )
    first = pre[:, :width]
    second = jax.nn.sigmoid(pre[:, width:])
    gated = (first * second).astype(jnp.bfloat16)
    upstream = cotangent[0, 0].astype(jnp.float32)
    dpre = jnp.concatenate(
        [upstream * second, upstream * first * second * (1.0 - second)], axis=1
    ).astype(jnp.bfloat16)
    grad_share = lax.psum_scatter(
        lax.dot_general(
            normed, dpre, (((0,), (0,)), ((), ())), preferred_element_type=jnp.float32
        ).astype(jnp.bfloat16),
        "fsdp",
        scatter_dimension=0,
        tiled=True,
    )
    return (gated[None, None], grad_share[None])


def kernel(
    n_dp, n_fsdp,
    frames_ref, route_ref, valid_ref, w_ref, cot_ref, gated_ref, grad_ref,
    frames_v, route_v, valid_v, cot_v, gated_v, out_v,
    sent, recv, normed, turned, w_all, dpre,
    mate_out, mate_in, peer_out, peer_in, own_out, own_in, own_sum,
    load_sem, self_sem, a2a_send, a2a_recv,
    w_send, w_recv, wm_send, wm_recv, wf_send, wf_recv,
    m_send, m_recv, p_send, p_recv, o_send, o_recv, g_sem, d_sem,
):
    f32, bf16 = jnp.float32, jnp.bfloat16
    me = lax.axis_index("dp")
    f = lax.axis_index("fsdp")
    mate = f + 1 - 2 * lax.rem(f, 2)
    peer = lax.rem(f + 2, n_fsdp)
    peer_mate = lax.rem(mate + 2, n_fsdp)
    rows, width = frames_v.shape
    block = rows // n_dp
    shard = w_ref.shape[0]
    part = shard // W_PARTS
    tiles = width // TILE

    barrier = pltpu.get_barrier_semaphore()
    for k in range(1, n_dp):
        pl.semaphore_signal(barrier, inc=1, device_id={"dp": lax.rem(me + k, n_dp)})
    pl.semaphore_signal(barrier, inc=1, device_id={"fsdp": mate})
    pl.semaphore_signal(barrier, inc=1, device_id={"fsdp": peer})

    loads = [
        pltpu.make_async_copy(route_ref, route_v, load_sem.at[0]),
        pltpu.make_async_copy(valid_ref, valid_v, load_sem.at[1]),
        pltpu.make_async_copy(frames_ref, frames_v, load_sem.at[2]),
        pltpu.make_async_copy(w_ref, w_all.at[pl.ds(pl.multiple_of(f * shard, shard), shard)], load_sem.at[3]),
        pltpu.make_async_copy(cot_ref, cot_v, load_sem.at[4]),
    ]
    for load in loads:
        load.start()

    def w_rows(owner, i):
        return pl.ds(pl.multiple_of(owner * shard + i * part, part), part)

    def w_to_peer(i):
        return pltpu.make_async_remote_copy(
            w_ref.at[pl.ds(i * part, part)], w_all.at[w_rows(f, i)],
            w_send.at[i], w_recv.at[i], device_id={"fsdp": peer})

    def w_to_mate(i):
        return pltpu.make_async_remote_copy(
            w_ref.at[pl.ds(i * part, part)], w_all.at[w_rows(f, i)],
            wm_send.at[i], wm_recv.at[i], device_id={"fsdp": mate})

    def w_onward(i):
        return pltpu.make_async_remote_copy(
            w_all.at[w_rows(peer, i)], w_all.at[w_rows(peer, i)],
            wf_send.at[i], wf_recv.at[i], device_id={"fsdp": mate})

    pl.semaphore_wait(barrier, n_dp + 1)
    for i in range(W_PARTS):
        w_to_peer(i).start()
    for i in range(W_PARTS):
        w_to_mate(i).start()

    for load in loads[:2]:
        load.wait()
    route = route_v[...]
    hit = lax.broadcasted_iota(jnp.int32, (rows, rows), 0) == route
    pick = jnp.where(hit, 1.0, 0.0).astype(bf16)
    real = jnp.where(valid_v[...] > 0, 1.0, 0.0).astype(bf16)
    keep = jnp.dot(jnp.broadcast_to(real, (16, rows)), pick, preferred_element_type=f32)[:1]
    pick = jnp.where(hit, keep, 0.0).astype(bf16)
    loads[2].wait()
    picked = lax.dot_general(
        pick, frames_v[...], (((0,), (0,)), ((), ())), preferred_element_type=f32)
    for t in range(n_dp):
        sent[t] = picked[t * block:(t + 1) * block].astype(bf16)

    def to_trainer(k):
        t = lax.rem(me + k, n_dp)
        return pltpu.make_async_remote_copy(
            sent.at[t], recv.at[me], a2a_send.at[t], a2a_recv.at[me], device_id={"dp": t})

    order = sorted(range(1, n_dp), key=lambda k: -min(k, n_dp - k))
    for k in order:
        to_trainer(k).start()
    stay = pltpu.make_async_copy(sent.at[me], recv.at[me], self_sem)
    stay.start()
    stay.wait()

    pairs = n_dp // 2

    def norm_pair(j):
        pair = lax.rem(me // 2 + j, pairs)
        for half in range(2):
            s = 2 * pair + half

            @pl.when(s != me)
            def _():
                pltpu.make_async_remote_copy(
                    sent.at[s], recv.at[s], a2a_send.at[s], a2a_recv.at[s], device_id={"dp": s}
                ).wait_recv()

        values = jnp.concatenate([recv[2 * pair].astype(f32), recv[2 * pair + 1].astype(f32)], axis=0)
        mean = jnp.mean(values, axis=-1, keepdims=True)
        centred = values - mean
        variance = jnp.mean(centred * centred, axis=-1, keepdims=True)
        at = pl.ds(pl.multiple_of(pair * 2 * block, 2 * block), 2 * block)
        normed[at, :] = (centred * lax.rsqrt(variance + 1e-05)).astype(bf16)

    for j in range(max(pairs, W_PARTS)):
        if j < W_PARTS:
            w_to_peer(j).wait_recv()
            w_onward(j).start()
        if j < pairs:
            norm_pair(j)
    for q in range(n_fsdp):
        turned[q] = normed[:, q * shard:(q + 1) * shard].T

    loads[3].wait()
    loads[4].wait()
    for i in range(W_PARTS):
        w_to_mate(i).wait_recv()
    for i in range(W_PARTS):
        w_onward(i).wait_recv()

    def mate_copy(i):
        return pltpu.make_async_remote_copy(
            mate_out.at[i], mate_in.at[i], m_send.at[i], m_recv.at[i], device_id={"fsdp": mate})

    def own_copy(i):
        return pltpu.make_async_remote_copy(
            own_out.at[i], own_in.at[i], o_send.at[i], o_recv.at[i], device_id={"fsdp": mate})

    def peer_copy(i):
        return pltpu.make_async_remote_copy(
            peer_out.at[i], peer_in.at[i], p_send.at[i], p_recv.at[i], device_id={"fsdp": peer})

    def gated_copy(i):
        cols = pl.ds(pl.multiple_of(i * TILE, TILE), TILE)
        return pltpu.make_async_copy(gated_v.at[:, cols], gated_ref.at[:, cols], g_sem.at[i])

    def partial(q):
        return jnp.dot(turned[q], dpre[...], preferred_element_type=f32)

    def tile(i, carry):
        lo = pl.ds(pl.multiple_of(i * TILE, TILE), TILE)
        hi = pl.ds(pl.multiple_of(width + i * TILE, TILE), TILE)
        rows_in = normed[...]
        first = jnp.dot(rows_in, w_all[:, lo], preferred_element_type=f32)
        second = jax.nn.sigmoid(jnp.dot(rows_in, w_all[:, hi], preferred_element_type=f32))
        upstream = cot_v[:, lo].astype(f32)
        gated_v[:, lo] = (first * second).astype(bf16)
        dpre[:, :TILE] = (upstream * second).astype(bf16)
        dpre[:, TILE:] = (upstream * first * second * (1.0 - second)).astype(bf16)
        gated_copy(i).start()
        mate_out[i] = partial(peer_mate).astype(bf16)
        mate_copy(i).start()
        chip_sum = partial(peer)
        own_out[i] = partial(mate).astype(bf16)
        own_copy(i).start()
        own_sum[i] = partial(f)
        mate_copy(i).wait_recv()
        peer_out[i] = (chip_sum + mate_in[i].astype(f32)).astype(bf16)
        peer_copy(i).start()
        return carry

    lax.fori_loop(0, tiles, tile, 0)

    def grad_copies(i):
        lo = pl.ds(pl.multiple_of(i * TILE, TILE), TILE)
        hi = pl.ds(pl.multiple_of(width + i * TILE, TILE), TILE)
        return (
            pltpu.make_async_copy(out_v.at[i, :, pl.ds(0, TILE)], grad_ref.at[:, lo], d_sem.at[i, 0]),
            pltpu.make_async_copy(out_v.at[i, :, pl.ds(TILE, TILE)], grad_ref.at[:, hi], d_sem.at[i, 1]),
        )

    def finish(i, carry):
        own_copy(i).wait_recv()
        half = own_sum[i] + own_in[i].astype(f32)
        peer_copy(i).wait_recv()
        out_v[i] = (half + peer_in[i].astype(f32)).astype(bf16)
        for copy in grad_copies(i):
            copy.start()
        return carry

    lax.fori_loop(0, tiles, finish, 0)

    for k in order:
        to_trainer(k).wait_send()
    for i in range(W_PARTS):
        w_to_peer(i).wait_send()
        w_to_mate(i).wait_send()
        w_onward(i).wait_send()

    def drain(i, carry):
        gated_copy(i).wait()
        mate_copy(i).wait_send()
        own_copy(i).wait_send()
        peer_copy(i).wait_send()
        for copy in grad_copies(i):
            copy.wait()
        return carry

    lax.fori_loop(0, tiles, drain, 0)


def fused(n_dp, n_fsdp, frames, route, valid, w_pw, cotangent):
    rows, width = frames.shape[2:]
    shard, wide = w_pw.shape
    block, tiles = rows // n_dp, width // TILE
    bf16, f32, i32 = jnp.bfloat16, jnp.float32, jnp.int32
    chunk = (tiles, shard, 2 * TILE)
    dma = pltpu.SemaphoreType.DMA
    scratch = [
        pltpu.VMEM((rows, width), bf16), pltpu.VMEM((1, rows), i32), pltpu.VMEM((1, rows), i32),
        pltpu.VMEM((rows, width), bf16), pltpu.VMEM((rows, width), bf16), pltpu.VMEM(chunk, bf16),
        pltpu.VMEM((n_dp, block, width), bf16), pltpu.VMEM((n_dp, block, width), bf16),
        pltpu.VMEM((rows, width), bf16), pltpu.VMEM((n_fsdp, shard, rows), bf16),
        pltpu.VMEM((width, wide), bf16), pltpu.VMEM((rows, 2 * TILE), bf16),
        *[pltpu.VMEM(chunk, bf16) for _ in range(6)], pltpu.VMEM(chunk, f32),
        dma((5,)), dma, dma((n_dp,)), dma((n_dp,)),
        *[dma((W_PARTS,)) for _ in range(6)],
        *[dma((tiles,)) for _ in range(7)], dma((tiles, 2)),
    ]
    macs = rows * width * wide * 2 + rows * rows * width
    gated, grad = pl.pallas_call(
        functools.partial(kernel, n_dp, n_fsdp),
        out_shape=(
            jax.ShapeDtypeStruct((rows, width), bf16),
            jax.ShapeDtypeStruct((shard, wide), bf16),
        ),
        in_specs=[pl.BlockSpec(memory_space=pl.ANY)] * 5,
        out_specs=[pl.BlockSpec(memory_space=pl.ANY)] * 2,
        scratch_shapes=scratch,
        cost_estimate=pl.CostEstimate(
            flops=2 * macs, bytes_accessed=(3 * rows * width + 2 * shard * wide) * 2,
            transcendentals=rows * width),
        compiler_params=pltpu.CompilerParams(
            collective_id=0, has_side_effects=True, vmem_limit_bytes=50 * 1024 * 1024),
    )(frames[0, 0], route[0], valid[0], w_pw, cotangent[0, 0])
    return (gated[None, None], grad[None])


def solution(mesh):
    n_dp, n_fsdp = mesh.shape["dp"], mesh.shape["fsdp"]

    def per_device(frames, route, valid, w_pw, cotangent):
        rows, width = frames.shape[2:]
        fits = (
            n_fsdp == 4 and n_dp % 2 == 0 and rows % (8 * n_dp) == 0
            and width % (n_fsdp * TILE) == 0 and w_pw.shape[0] % (16 * W_PARTS) == 0
        )
        if fits:
            return fused(n_dp, n_fsdp, frames, route, valid, w_pw, cotangent)
        return plain(frames, route, valid, w_pw, cotangent)

    in_specs = (
        P("dp", "fsdp", None, None),
        P("dp", "fsdp", None),
        P("dp", "fsdp", None),
        P("fsdp", None),
        P("dp", "fsdp", None, None),
    )
    out_specs = (P("dp", "fsdp", None, None), P("dp", "fsdp", None))
    return jax.shard_map(
        per_device, mesh=mesh, in_specs=in_specs, out_specs=out_specs, check_vma=False
    )
```
